128 devices in a mesh: replica: 16 (over z_hi, y, core), shard: 8 (over x, z_lo).
Axes of the slice: x: 4, y: 4, z: 4 (z_hi: 2, z_lo: 2; z = z_hi * 2 + z_lo), core: 2. Of those that a mesh axis runs over, the one named last changes fastest.
Arguments:
- student_ctx: bfloat16 [163840, 1536], P(('replica', 'shard')), may hold values from -24 to 24
- out_grad: bfloat16 [163840, 1536], P(('replica', 'shard')), may hold values from -0.015625 to 0.015625
- weight: float32 [1536, 1536], P('shard'), may hold values from -0.15625 to 0.15625
- moment_one: float32 [1536, 1536], P('shard'), may hold values from -6 to 6
- moment_two: float32 [1536, 1536], P('shard'), may hold values from 0.05 to 2
- teacher: float32 [1536, 1536], P('shard'), may hold values from -0.15625 to 0.15625
- teach_input: bfloat16 [65536, 1536], P(('replica', 'shard')), may hold values from -6 to 6
- teach_ctx: bfloat16 [65536, 1536], P(('replica', 'shard')), may hold values from -6 to 6
Outputs:
- ctx_grad: bfloat16 [163840, 1536], P(('replica', 'shard'))
- weight_next: float32 [1536, 1536], P('shard')
- moment_one_next: float32 [1536, 1536], P('shard')
- moment_two_next: float32 [1536, 1536], P('shard')
- teacher_next: float32 [1536, 1536], P('shard')
- teacher_out: bfloat16 [65536, 1536], P(('replica', 'shard'))
The draws below stay inside these ranges and needn't reach their ends.
All inputs are finite; a program needn't handle non-finite values.
Results may differ from the reference program's by a relative error of at most 0.0043.
The reference program's roundings to bfloat16 on the way (of `weight_half` and `teacher_half`) count: a program that leaves them out, or rounds other values in their place, can miss the bound.
Values may be sent and summed in bfloat16 or wider, within the bound.
A program may use at most 192 MiB of HBM per device.

```python
import math
import jax
import jax.numpy as jnp
from jax import lax

D = 1536
STEP = 100
TOKENS = 163840
TEACH_TOKENS = 65536


def with_spikes(result, key, source, target, shards_of, factor):
    owner, partner = [(jnp.arange(result.shape[axis_at]) // (result.shape[axis_at] // shards_of)).reshape([-1 if axis == axis_at else 1 for axis in range(result.ndim)]) for axis_at in (source, target)]
    chosen = jax.random.permutation(key, shards_of)[partner]
    strong = (owner == chosen) | (owner == (partner + shards_of // 2) % shards_of)
    return jnp.where(strong, factor * result, result)


def levels(key, extent, split, smallest, high):
    level = 1.0
    for dim, parts in split:
        heights = jax.random.uniform(jax.random.fold_in(jax.random.fold_in(key, 6), dim), (parts,), jnp.float32, smallest / len(split), high / len(split))
        level = level * jnp.repeat(jnp.exp(heights), extent[dim] // parts).reshape((-1,) + (1,) * (len(extent) - 1 - dim))
    return level


def scatter_about(stream_key, dims, deviation, limit, split=(), kind=jnp.bfloat16):
    values = deviation * jax.random.normal(stream_key, dims, jnp.float32)
    if split:
        values = values * levels(stream_key, dims, split, -0.22, 0.18)
    return jnp.clip(values, -limit, limit).astype(kind)


def noise_with(key, extent, width, bound, shards, heavy, kind=jnp.bfloat16):
    drawn = width * jax.random.normal(key, extent, jnp.float32)
    if shards:
        drawn = drawn * levels(key, extent, shards, -0.22, 0.18)
    return jnp.clip(with_spikes(drawn, jax.random.fold_in(key, 3), *heavy), -bound, bound).astype(kind)


def setup_inputs(seed: int = 0) -> dict:
    keys = jax.random.split(jax.random.key(seed), 9)
    return {
        "student_ctx": noise_with(keys[0], (TOKENS, D), 1.0, 24.0, ((0, 128),), (0, 1, 128, 5.5)),
        "out_grad": scatter_about(keys[1], (TOKENS, D), TOKENS ** -0.5, 0.015625, ((0, 128),)),
        "weight": scatter_about(keys[2], (D, D), D ** -0.5, 0.15625, ((0, 8),), jnp.float32),
        "moment_one": scatter_about(keys[3], (D, D), 1.0, 6.0, ((0, 8),), jnp.float32),
        "moment_two": jnp.clip(jnp.exp(math.log(2.0) - 3.6888794 * jax.random.uniform(keys[4], (D, D), jnp.float32) ** levels(keys[4], (D, D), ((0, 8),), -0.2, 0.2)), 0.05, 2.0),
        "teacher": scatter_about(keys[5], (D, D), D ** -0.5, 0.15625, ((0, 8),), jnp.float32),
        "teach_input": scatter_about(keys[6], (TEACH_TOKENS, D), 1.0, 6.0, ((0, 128),)),
        "teach_ctx": scatter_about(keys[7], (TEACH_TOKENS, D), 1.0, 6.0, ((0, 128),)),
    }


beta_one = 0.9
beta_two = 0.999
adam_eps = 1e-08
learn_rate = 0.001
decay_rate = 0.04
momentum = 0.994

def reference(student_ctx, out_grad, weight, moment_one, moment_two, teacher, teach_input, teach_ctx):
    weight_half = weight.astype(jnp.bfloat16)
    teacher_next = momentum * teacher + (1.0 - momentum) * weight
    teacher_half = teacher_next.astype(jnp.bfloat16)
    projected = jnp.dot(teach_ctx, teacher_half, preferred_element_type=jnp.float32)
    teacher_out = (teach_input.astype(jnp.float32) + projected).astype(jnp.bfloat16)
    ctx_grad = lax.dot_general(out_grad, weight_half, (((1,), (1,)), ((), ())), preferred_element_type=jnp.float32).astype(jnp.bfloat16)
    gradient = lax.dot_general(student_ctx, out_grad, (((0,), (0,)), ((), ())), preferred_element_type=jnp.float32)
    moment_one_next = beta_one * moment_one + (1.0 - beta_one) * gradient
    moment_two_next = beta_two * moment_two + (1.0 - beta_two) * gradient * gradient
    correct_one = 1.0 - beta_one ** STEP
    correct_two = 1.0 - beta_two ** STEP
    update = moment_one_next / correct_one / (jnp.sqrt(moment_two_next / correct_two) + adam_eps) + decay_rate * weight
    weight_next = weight - learn_rate * update
    return (ctx_grad, weight_next, moment_one_next, moment_two_next, teacher_next, teacher_out)
```

```python
import jax
import jax.numpy as jnp
from jax import lax
from jax.experimental import pallas as pl
from jax.experimental.pallas import tpu as pltpu
from jax.sharding import PartitionSpec as P

STEP = 100


beta_one = 0.9
beta_two = 0.999
adam_eps = 1e-08
learn_rate = 0.001
decay_rate = 0.04
momentum = 0.994

F32 = jnp.float32
BF16 = jnp.bfloat16
MESH = pl.DeviceIdType.MESH

D = 1536
HALF = D // 2
SHARD_ROWS = 192
PIECE_HALF = 96
BLOCK = 48
TOKENS = 1280
TEACH = 512

X1, X2, ZW, CF = 0, 4, 6, 14
PAIR = CF + 14
YA = PAIR + 4
YB = YA + 8
XG = YB + 8
ZG = XG + 3
YG = ZG + 3
CG = YG + 3
N_COPIES = CG + 4


def kernel(
    student_ctx, out_grad, weight, teacher, teach_input, teach_ctx,
    ctx_grad, teacher_out, gradient,
    ctx_v, og_v, w_v, t_v, tin_v, tctx_v,
    mats, g_peer, g_own, g_recv,
    ya_s, ya_r, yb_s, yb_r, xg_s, xg_r, zg_s, zg_r, rows_v,
    cg_v, to_v,
    send_sem, recv_sem, in_sem, out_sem,
):
    replica, shard = lax.axis_index("replica"), lax.axis_index("shard")
    core, y = replica % 2, (replica // 2) % 4
    z = (replica // 8) * 2 + shard % 2
    x, parity = shard // 2, shard % 2
    other = 1 - core

    def device(dx=0, dy=0, dz=0, flip=False):
        xx, yy, zz = (x + dx) % 4, (y + dy) % 4, (z + dz) % 4
        cc = other if flip else core
        return {"replica": ((zz // 2) * 4 + yy) * 2 + cc, "shard": xx * 2 + zz % 2}

    partners = [device(flip=True)]
    for step in (1, 2, 3):
        partners += [device(dx=step), device(dy=step), device(dz=step)]
    barrier = pltpu.get_barrier_semaphore()
    for partner in partners:
        pl.semaphore_signal(barrier, inc=1, device_id=partner, device_id_type=MESH)

    loads = [
        pltpu.make_async_copy(src, dst, in_sem.at[i])
        for i, (src, dst) in enumerate(
            [(weight, w_v), (teacher, t_v), (out_grad, og_v), (student_ctx, ctx_v), (teach_ctx, tctx_v), (teach_input, tin_v)]
        )
    ]
    for load in loads:
        load.start()

    copies = {}

    def send(i, src, dst, target):
        copies[i] = pltpu.make_async_remote_copy(
            src_ref=src, dst_ref=dst, send_sem=send_sem.at[i], recv_sem=recv_sem.at[i],
            device_id=target, device_id_type=MESH,
        )
        copies[i].start()

    def arrived(*ids):
        for i in ids:
            copies[i].wait_recv()

    loads[0].wait()
    loads[1].wait()
    for r in range(0, SHARD_ROWS, BLOCK):
        rows = pl.ds(r, BLOCK)
        w = w_v[rows, :]
        mats[0, shard, rows, :] = w.astype(BF16)
        mats[1, shard, rows, :] = (momentum * t_v[rows, :] + (1.0 - momentum) * w).astype(BF16)

    pl.semaphore_wait(barrier, len(partners))

    def piece(dx, half, dparity=False):
        index = ((x + dx) % 4) * 2 + ((1 - parity) if dparity else parity)
        return mats.at[core, index, pl.ds(half * PIECE_HALF, PIECE_HALF)]

    def send_piece(i, ref, target):
        send(i, ref, ref, target)

    right, left, up, down = device(dx=1), device(dx=3), device(dz=1), device(dz=3)
    twin = device(flip=True)
    offsets = (0, 3, 1, 2)

    def send_z(j, half):
        send_piece(ZW + 2 * j + half, piece(offsets[j], half), up if half == 0 else down)

    def hand_over(slot, dx, half, dparity=False):
        send_piece(CF + slot, piece(dx, half, dparity), twin)

    send_piece(X1 + 0, piece(0, 0), right)
    send_piece(X1 + 2, piece(0, 1), left)
    send_z(0, 0)
    send_z(0, 1)

    north, south, far_y = device(dy=1), device(dy=3), (y + 2) % 4
    y_up, y_down = (y + 1) % 4, (y + 3) % 4

    loads[2].wait()
    loads[3].wait()

    def grad_chunk(k):
        columns = ctx_v[:, pl.ds(pl.multiple_of(((x + 1 + k) % 4) * 384, 128), 384)]

        def part(side):
            return lax.dot_general(
                columns, og_v[:, pl.ds(pl.multiple_of(side * HALF, 128), HALF)],
                (((0,), (0,)), ((), ())), preferred_element_type=F32,
            )

        g_peer[k] = part(other)
        send(PAIR + k, g_peer.at[k], g_recv.at[k], twin)
        g_own[k] = part(core)

    def block(k, par, yy):
        return g_own[k, pl.ds(pl.multiple_of(par * SHARD_ROWS + yy * BLOCK, 16), BLOCK), :]

    def y_first(k):
        arrived(PAIR + k)
        g_own[k] = g_own[k] + g_recv[k]
        ya_s[k, 0] = block(k, 0, far_y).astype(BF16)
        ya_s[k, 1] = block(k, 1, far_y).astype(BF16)
        send(YA + 2 * k, ya_s.at[k, 0], ya_r.at[k, 0], north)
        send(YA + 2 * k + 1, ya_s.at[k, 1], ya_r.at[k, 1], south)

    def y_second(k):
        yb_s[k, 0, 1] = block(k, 1, y_up).astype(BF16)
        yb_s[k, 1, 0] = block(k, 0, y_down).astype(BF16)
        arrived(YA + 2 * k, YA + 2 * k + 1)
        yb_s[k, 0, 0] = (block(k, 0, y_up) + ya_r[k, 0].astype(F32)).astype(BF16)
        yb_s[k, 1, 1] = (block(k, 1, y_down) + ya_r[k, 1].astype(F32)).astype(BF16)
        send(YB + 2 * k, yb_s.at[k, 0], yb_r.at[k, 0], north)
        send(YB + 2 * k + 1, yb_s.at[k, 1], yb_r.at[k, 1], south)

    def y_sum(k, par):
        return block(k, par, y) + yb_r[k, 0, par].astype(F32) + yb_r[k, 1, par].astype(F32)

    def y_third(k):
        arrived(YB + 2 * k, YB + 2 * k + 1)
        for par in (0, 1):
            xg_s[k, par] = y_sum(k, par).astype(BF16)
        send(XG + k, xg_s.at[k], xg_r.at[k], device(dx=1 + k))

    stores = []

    def store(src, dst):
        copy = pltpu.make_async_copy(src, dst, out_sem.at[len(stores)])
        copy.start()
        stores.append(copy)

    def ctx_columns(slot, dx):
        pair = (x + dx) % 4
        rows = mats[0, pl.ds(pair * 2, 2)].reshape(2 * SHARD_ROWS, D)

        def step(m, _):
            tokens = pl.ds(pl.multiple_of(m * 640, 128), 640)
            cg_v[slot, tokens, :] = lax.dot_general(
                og_v[tokens, :], rows, (((1,), (1,)), ((), ())), preferred_element_type=F32
            ).astype(BF16)
            return 0

        lax.fori_loop(0, TOKENS // 640, step, 0)
        store(cg_v.at[slot], ctx_grad.at[:, pl.ds(pl.multiple_of(pair * 384, 128), 384)])

    grad_chunk(0)
    grad_chunk(1)
    y_first(0)
    grad_chunk(2)
    y_first(1)
    y_second(0)
    grad_chunk(3)
    y_first(2)
    y_second(1)
    arrived(X1 + 0, X1 + 2)
    send_piece(X1 + 1, piece(0, 1), right)
    send_piece(X1 + 3, piece(0, 0), left)
    send_piece(X2 + 0, piece(3, 0), right)
    send_piece(X2 + 1, piece(1, 1), left)
    send_z(1, 0)
    send_z(2, 1)
    hand_over(0, 3, 0)
    hand_over(1, 1, 1)
    y_first(3)
    y_second(2)
    arrived(ZW + 0, ZW + 1)
    hand_over(2, 0, 0, True)
    hand_over(3, 0, 1, True)
    y_second(3)
    y_third(0)
    arrived(X1 + 1, X1 + 3)
    send_z(1, 1)
    send_z(2, 0)
    hand_over(4, 3, 1)
    hand_over(5, 1, 0)
    arrived(CF + 2, CF + 3)
    ctx_columns(0, 0)
    arrived(ZW + 2, ZW + 5)
    hand_over(6, 3, 0, True)
    hand_over(7, 1, 1, True)
    y_third(1)
    arrived(X2 + 0, X2 + 1)
    send_z(3, 0)
    send_z(3, 1)
    hand_over(8, 2, 0)
    hand_over(9, 2, 1)
    y_third(2)
    arrived(ZW + 3, ZW + 4)
    hand_over(10, 3, 1, True)
    hand_over(11, 1, 0, True)
    arrived(CF + 0, CF + 5, CF + 4, CF + 1, CF + 6, CF + 7, CF + 10, CF + 11)
    arrived(YB + 6, YB + 7, XG + 0, XG + 1, XG + 2)
    for par in (0, 1):
        total = y_sum(3, par)
        for k in range(3):
            total = total + xg_r[k, par].astype(F32)
        zg_s[par] = total
    send(ZG + 0, zg_s.at[1 - parity], zg_r.at[z], up)
    send(ZG + 1, zg_s.at[1 - parity], zg_r.at[z], down)
    send(ZG + 2, zg_s.at[parity], zg_r.at[z], device(dz=2))
    zg_r[z] = zg_s[parity]
    ctx_columns(1, 3)
    ctx_columns(2, 1)
    arrived(ZW + 6, ZW + 7)
    hand_over(12, 2, 0, True)
    hand_over(13, 2, 1, True)
    arrived(ZG + 0, ZG + 1, ZG + 2)
    rows_v[y, core] = (zg_r[0] + zg_r[1] + zg_r[2] + zg_r[3]).astype(BF16)
    own = rows_v.at[y, core]
    send(YG + 0, own, own, north)
    send(YG + 1, own, own, south)
    send(YG + 2, own, own, device(dy=2))
    send(CG + 0, own, own, twin)
    arrived(CF + 8, CF + 9, CF + 12, CF + 13)
    ctx_columns(3, 2)
    for j, source in enumerate((y_down, y_up, far_y)):
        arrived(YG + j)
        got = rows_v.at[source, core]
        send(CG + 1 + j, got, got, twin)
    loads[4].wait()
    loads[5].wait()

    def teach(n, _):
        columns = pl.ds(pl.multiple_of(n * 768, 128), 768)
        projected = jnp.dot(tctx_v[...], mats[1, :, :, columns].reshape(D, 768), preferred_element_type=F32)
        to_v[:, columns] = (tin_v[:, columns].astype(F32) + projected).astype(BF16)
        return 0

    lax.fori_loop(0, 2, teach, 0)
    store(to_v, teacher_out)
    arrived(CG + 0, CG + 1, CG + 2, CG + 3)
    for yy in range(4):
        for cc in range(2):
            store(rows_v.at[yy, cc], gradient.at[pl.ds(yy * BLOCK, BLOCK), pl.ds(cc * HALF, HALF)])
    for i in range(N_COPIES):
        copies[i].wait_send()
    for copy in stores:
        copy.wait()


def communicate(student_ctx, out_grad, weight, teacher, teach_input, teach_ctx):
    anywhere = pl.BlockSpec(memory_space=pl.ANY)
    vmem = pltpu.VMEM
    return pl.pallas_call(
        kernel,
        out_shape=(
            jax.ShapeDtypeStruct((TOKENS, D), BF16),
            jax.ShapeDtypeStruct((TEACH, D), BF16),
            jax.ShapeDtypeStruct((SHARD_ROWS, D), BF16),
        ),
        in_specs=[anywhere] * 6,
        out_specs=(anywhere,) * 3,
        scratch_shapes=[
            vmem((TOKENS, D), BF16),
            vmem((TOKENS, D), BF16),
            vmem((SHARD_ROWS, D), F32),
            vmem((SHARD_ROWS, D), F32),
            vmem((TEACH, D), BF16),
            vmem((TEACH, D), BF16),
            vmem((2, 8, SHARD_ROWS, D), BF16),
            vmem((4, 384, HALF), F32),
            vmem((4, 384, HALF), F32),
            vmem((4, 384, HALF), F32),
            vmem((4, 2, BLOCK, HALF), BF16),
            vmem((4, 2, BLOCK, HALF), BF16),
            vmem((4, 2, 2, BLOCK, HALF), BF16),
            vmem((4, 2, 2, BLOCK, HALF), BF16),
            vmem((3, 2, BLOCK, HALF), BF16),
            vmem((3, 2, BLOCK, HALF), BF16),
            vmem((2, BLOCK, HALF), F32),
            vmem((4, BLOCK, HALF), F32),
            vmem((4, 2, BLOCK, HALF), BF16),
            vmem((4, TOKENS, 384), BF16),
            vmem((TEACH, D), BF16),
            pltpu.SemaphoreType.DMA((N_COPIES,)),
            pltpu.SemaphoreType.DMA((N_COPIES,)),
            pltpu.SemaphoreType.DMA((6,)),
            pltpu.SemaphoreType.DMA((13,)),
        ],
        compiler_params=pltpu.CompilerParams(
            collective_id=0, has_side_effects=True, vmem_limit_bytes=62 * 2**20
        ),
        cost_estimate=pl.CostEstimate(
            flops=2 * D * D * (2 * TOKENS + TEACH), bytes_accessed=22 * 2**20, transcendentals=0
        ),
        name="exchange",
    )(student_ctx, out_grad, weight, teacher, teach_input, teach_ctx)


def body(student_ctx, out_grad, weight, moment_one, moment_two, teacher, teach_input, teach_ctx):
    ctx_grad, teacher_out, own_rows = communicate(
        student_ctx, out_grad, weight, teacher, teach_input, teach_ctx
    )
    teacher_next = momentum * teacher + (1.0 - momentum) * weight
    gradient = own_rows.astype(F32)
    moment_one_next = beta_one * moment_one + (1.0 - beta_one) * gradient
    moment_two_next = beta_two * moment_two + (1.0 - beta_two) * gradient * gradient
    correct_one = 1.0 - beta_one**STEP
    correct_two = 1.0 - beta_two**STEP
    update = (
        moment_one_next / correct_one / (jnp.sqrt(moment_two_next / correct_two) + adam_eps)
        + decay_rate * weight
    )
    weight_next = weight - learn_rate * update
    return (ctx_grad, weight_next, moment_one_next, moment_two_next, teacher_next, teacher_out)


def solution(mesh):
    return jax.shard_map(
        body,
        mesh=mesh,
        in_specs=(
            P(("replica", "shard"), None),
            P(("replica", "shard"), None),
            P("shard", None),
            P("shard", None),
            P("shard", None),
            P("shard", None),
            P(("replica", "shard"), None),
            P(("replica", "shard"), None),
        ),
        out_specs=(
            P(("replica", "shard"), None),
            P("shard", None),
            P("shard", None),
            P("shard", None),
            P("shard", None),
            P(("replica", "shard"), None),
        ),
        check_vma=False,
    )
```

```python
import jax
import jax.numpy as jnp
from jax import lax
from jax.experimental import pallas as pl
from jax.experimental.pallas import tpu as pltpu
from jax.sharding import PartitionSpec as P

STEP = 100


beta_one = 0.9
beta_two = 0.999
adam_eps = 1e-08
learn_rate = 0.001
decay_rate = 0.04
momentum = 0.994

F32 = jnp.float32
BF16 = jnp.bfloat16
MESH = pl.DeviceIdType.MESH

D = 1536
HALF = D // 2
SHARD_ROWS = 192
PIECE_HALF = 96
BLOCK = 48
TOKENS = 1280
TEACH = 512

THIRD = 256
ORDER = (2, 1, 3, 0)
LANES = 128

sizes = dict(
    X1=6, X2=2, ZW=8, YW=10, CF=14, PAIR=4,
    Y1=12, Z1=12, XA=3, XB=3, ZB=3, YB=3, ZC=3, YC=3, XC=3, GA=7, GC=8,
)
first = {}
N_COPIES = 0
for name, size in sizes.items():
    first[name] = N_COPIES
    N_COPIES += size


def kernel(
    student_ctx, out_grad, weight, teacher, teach_input, teach_ctx,
    ctx_grad, teacher_out, gradient,
    ctx_v, og_v, w_v, t_v, tin_v, tctx_v,
    mats, g_peer, g_own, g_recv,
    y1_s, y1_r, z1_s, z1_r, xa_s, xa_r,
    xb_s, xb_r, zb_s, zb_r, yb_s, yb_r,
    zc_s, zc_r, yc_s, yc_r, xc_s, xc_r,
    rows_v, sum_v,
    send_sem, recv_sem, in_sem,
):
    replica, shard = lax.axis_index("replica"), lax.axis_index("shard")
    core, y = replica % 2, (replica // 2) % 4
    z_high = replica // 8
    z = z_high * 2 + shard % 2
    x, parity = shard // 2, shard % 2
    other = 1 - core
    h = y % 2

    def device(dx=0, dy=0, dz=0, flip=False):
        xx, yy, zz = (x + dx) % 4, (y + dy) % 4, (z + dz) % 4
        cc = other if flip else core
        return {"replica": ((zz // 2) * 4 + yy) * 2 + cc, "shard": xx * 2 + zz % 2}

    partners = [device(flip=True)]
    for step in (1, 2, 3):
        partners += [device(dx=step), device(dy=step), device(dz=step), device(dy=step, dz=2)]
    barrier = pltpu.get_barrier_semaphore()
    for partner in partners:
        pl.semaphore_signal(barrier, inc=1, device_id=partner, device_id_type=MESH)

    def ctx_columns_at(k):
        return pl.ds(pl.multiple_of(((x + ORDER[k]) % 4) * 384, 128), 384)

    pairs = [(weight, w_v), (teacher, t_v), (out_grad, og_v)]
    pairs += [(student_ctx.at[:, ctx_columns_at(k)], ctx_v.at[k]) for k in range(4)]
    pairs += [(teach_ctx, tctx_v), (teach_input, tin_v)]
    loads = [pltpu.make_async_copy(src, dst, in_sem.at[i]) for i, (src, dst) in enumerate(pairs)]
    for i in range(4):
        loads[i].start()

    copies = {}

    def send(name, i, src, dst, target):
        copies[name, i] = pltpu.make_async_remote_copy(
            src_ref=src, dst_ref=dst,
            send_sem=send_sem.at[first[name] + i], recv_sem=recv_sem.at[first[name] + i],
            device_id=target, device_id_type=MESH,
        )
        copies[name, i].start()

    def arrived(name, *ids):
        for i in ids:
            copies[name, i].wait_recv()

    loads[0].wait()
    loads[1].wait()
    for r in range(0, SHARD_ROWS, BLOCK):
        rows = pl.ds(r, BLOCK)
        w = w_v[rows, :]
        mats[0, shard, rows, :] = w.astype(BF16)
        mats[1, shard, rows, :] = (momentum * t_v[rows, :] + (1.0 - momentum) * w).astype(BF16)

    for i in range(4, 9):
        loads[i].start()
    pl.semaphore_wait(barrier, len(partners))

    right, left, up, down = device(dx=1), device(dx=3), device(dz=1), device(dz=3)
    north, south, twin = device(dy=1), device(dy=3), device(flip=True)
    offsets = (0, 3, 1, 2)

    def piece(dx, start, size, flipped):
        index = ((x + dx) % 4) * 2 + ((1 - parity) if flipped else parity)
        return mats.at[core, index, pl.ds(pl.multiple_of(start, 16), size)]

    def half(dx, near, flipped=False):
        return piece(dx, (h if near else 1 - h) * 96, 96, flipped)

    def quarter(dx, q, flipped=False):
        return piece(dx, h * 96 + q * 48, 48, flipped)

    def pass_on(name, i, ref, target):
        send(name, i, ref, ref, target)

    def send_z(j, q):
        pass_on("ZW", 2 * j + q, quarter(offsets[j], q), up if q == 0 else down)

    def send_y(j, q):
        ref = quarter(offsets[j], q, True) if j < 4 else quarter(2, q)
        pass_on("YW", 2 * j + q, ref, north if q == 0 else south)

    def hand_over(slot, ref):
        pass_on("CF", slot, ref, twin)

    def z_event(j):
        arrived("ZW", 2 * j, 2 * j + 1)
        send_y(j, 0)
        send_y(j, 1)
        hand_over(6 + 2 * j, half(offsets[j], True, True))

    def y_event(j):
        arrived("YW", 2 * j, 2 * j + 1)
        if j < 4:
            hand_over(7 + 2 * j, half(offsets[j], False, True))
        else:
            hand_over(5, half(2, False))

    pass_on("X1", 0, quarter(0, 0), right)
    pass_on("X1", 1, quarter(0, 1), left)
    pass_on("X1", 2, quarter(0, 1), right)
    pass_on("X1", 3, quarter(0, 0), left)
    send_z(0, 0)
    send_z(0, 1)

    def grad_part(k, side):
        return lax.dot_general(
            ctx_v[k], og_v[:, pl.ds(pl.multiple_of(side * HALF, 128), HALF)],
            (((0,), (0,)), ((), ())), preferred_element_type=F32,
        )

    def grad_peer(k):
        loads[3 + k].wait()
        g_peer[k] = grad_part(k, other)
        send("PAIR", k, g_peer.at[k], g_recv.at[k], twin)

    def grad_own(k):
        g_own[k] = grad_part(k, core)

    def both(k, row, n_rows, column, n_columns):
        at = (k, pl.ds(pl.multiple_of(row, 16), n_rows), pl.ds(pl.multiple_of(column, 128), n_columns))
        return g_own[at] + g_recv[at]

    def phase_one(k):
        arrived("PAIR", k)
        if k < 3:
            xa_s[k] = both(k, 0, 384, THIRD, THIRD).astype(BF16)
            send("XA", k, xa_s.at[k], xa_r.at[k], device(dx=ORDER[k]))
        for j in range(3):
            yy = (y + 1 + j) % 4
            for par in (0, 1):
                y1_s[k, j, par] = both(k, par * SHARD_ROWS + yy * BLOCK, BLOCK, 0, THIRD).astype(BF16)
            send("Y1", 3 * k + j, y1_s.at[k, j], y1_r.at[k, j], device(dy=1 + j))
            zz = (z + 1 + j) % 4
            z1_s[k, j] = both(
                k, (zz % 2) * SHARD_ROWS, SHARD_ROWS, 2 * THIRD + (zz // 2) * LANES, LANES
            ).astype(BF16)
            send("Z1", 3 * k + j, z1_s.at[k, j], z1_r.at[k, j], device(dz=1 + j))

    def first_y(k):
        arrived("Y1", 3 * k, 3 * k + 1, 3 * k + 2)
        for par in (0, 1):
            total = both(k, par * SHARD_ROWS + y * BLOCK, BLOCK, 0, THIRD)
            for j in range(3):
                total = total + y1_r[k, j, par].astype(F32)
            xb_s[k, par] = total
        if k < 3:
            send("XB", k, xb_s.at[k], xb_r.at[k], device(dx=ORDER[k]))

    def first_z(k):
        arrived("Z1", 3 * k, 3 * k + 1, 3 * k + 2)
        for yy in range(4):
            rows = pl.ds(yy * BLOCK, BLOCK)
            total = both(k, parity * SHARD_ROWS + yy * BLOCK, BLOCK, 2 * THIRD + z_high * LANES, LANES)
            for j in range(3):
                total = total + z1_r[k, j, rows, :].astype(F32)
            yb_s[yy, k] = total

    def first_x():
        arrived("XA", 0, 1, 2)
        for par in (0, 1):
            for zh in (0, 1):
                for q in range(4):
                    rows = pl.ds(par * SHARD_ROWS + q * BLOCK, BLOCK)
                    lanes = pl.ds(zh * LANES, LANES)
                    total = both(3, par * SHARD_ROWS + q * BLOCK, BLOCK, THIRD + zh * LANES, LANES)
                    for k in range(3):
                        total = total + xa_r[k, rows, lanes].astype(F32)
                    zb_s[par, zh, q * BLOCK:(q + 1) * BLOCK, :] = total
        for j in range(3):
            zz = (z + 1 + j) % 4
            send("ZB", j, zb_s.at[zz % 2, zz // 2], zb_r.at[j], device(dz=1 + j))

    def second_y():
        for j in range(3):
            send("YB", j, yb_s.at[(y + 1 + j) % 4], yb_r.at[j], device(dy=1 + j))

    def third_z():
        arrived("XB", 0, 1, 2)
        for par in (0, 1):
            for zh in (0, 1):
                lanes = pl.ds(zh * LANES, LANES)
                zc_s[par, zh] = (
                    xb_s[3, par, :, lanes] + xb_r[0, par, :, lanes] + xb_r[1, par, :, lanes] + xb_r[2, par, :, lanes]
                )
        for j in range(3):
            zz = (z + 1 + j) % 4
            send("ZC", j, zc_s.at[zz % 2, zz // 2], zc_r.at[j], device(dz=1 + j))

    def third_y():
        arrived("ZB", 0, 1, 2)
        for yy in range(4):
            rows = pl.ds(yy * BLOCK, BLOCK)
            yc_s[yy] = zb_s[parity, z_high, rows, :] + zb_r[0, rows, :] + zb_r[1, rows, :] + zb_r[2, rows, :]
        for j in range(3):
            send("YC", j, yc_s.at[(y + 1 + j) % 4], yc_r.at[j], device(dy=1 + j))

    def third_x():
        arrived("YB", 0, 1, 2)
        for k in range(4):
            xc_s[k] = yb_s[y, k] + yb_r[0, k] + yb_r[1, k] + yb_r[2, k]
        for k in range(3):
            send("XC", k, xc_s.at[k], xc_r.at[k], device(dx=ORDER[k]))

    steps = [(0, 1), (0, 3), (0, 2), (2, 0), (2, 1), (2, 3), (2, 2)]

    def share():
        arrived("ZC", 0, 1, 2)
        rows_v[z_high, y, core, 0] = (
            zc_s[parity, z_high] + zc_r[0] + zc_r[1] + zc_r[2]
        ).astype(BF16)
        arrived("YC", 0, 1, 2)
        rows_v[z_high, y, core, 1] = (yc_s[y] + yc_r[0] + yc_r[1] + yc_r[2]).astype(BF16)
        arrived("XC", 0, 1, 2)
        rows_v[z_high, y, core, 2] = (xc_s[3] + xc_r[0] + xc_r[1] + xc_r[2]).astype(BF16)
        own = rows_v.at[z_high, y, core]
        for i, (dz, dy) in enumerate(steps):
            send("GA", i, own, own, device(dy=dy, dz=dz))
        send("GC", 7, own, own, twin)

    def share_on():
        for i, (dz, dy) in enumerate(steps):
            arrived("GA", i)
            got = rows_v.at[(z_high + dz // 2) % 2, (y + 4 - dy) % 4, core]
            send("GC", i, got, got, twin)

    def place(zh, yy):
        for cc in range(2):
            for third in range(3):
                start = cc * HALF + third * THIRD + zh * LANES
                gradient[yy * BLOCK:(yy + 1) * BLOCK, start:start + LANES] = rows_v[zh, yy, cc, third]

    def columns_of(dx):
        return pl.ds(pl.multiple_of(((x + dx) % 4) * 384, 128), 384)

    def pieces_of(m, dx):
        return mats[m, pl.ds(((x + dx) % 4) * 2, 2)].reshape(2 * SHARD_ROWS, D)

    def ctx_work(dx):
        ctx_grad[:, columns_of(dx)] = lax.dot_general(
            og_v[...], pieces_of(0, dx), (((1,), (1,)), ((), ())), preferred_element_type=F32
        ).astype(BF16)

    def teach_part(dx, at):
        return jnp.dot(
            tctx_v[:, columns_of(dx)], mats[1, pl.ds(((x + dx) % 4) * 2, 2), :, at].reshape(2 * SHARD_ROWS, HALF),
            preferred_element_type=F32,
        )

    def teach_most():
        def step(n, _):
            at = pl.ds(pl.multiple_of(n * HALF, 128), HALF)
            sum_v[:, at] = teach_part(0, at) + teach_part(3, at) + teach_part(1, at)
            return 0

        lax.fori_loop(0, 2, step, 0)

    def teach_rest():
        def step(n, _):
            at = pl.ds(pl.multiple_of(n * HALF, 128), HALF)
            teacher_out[:, at] = (tin_v[:, at].astype(F32) + (sum_v[:, at] + teach_part(2, at))).astype(BF16)
            return 0

        lax.fori_loop(0, 2, step, 0)

    def x_event_first():
        arrived("X1", 0, 1)
        pass_on("X2", 0, quarter(3, 0), right)
        pass_on("X2", 1, quarter(1, 1), left)
        send_z(1, 0)
        send_z(2, 1)

    def x_event_second():
        arrived("X1", 2, 3)
        send_z(1, 1)
        send_z(2, 0)
        hand_over(0, half(3, True))
        hand_over(1, half(1, True))

    def opposite_event():
        arrived("X2", 0, 1)
        send_z(3, 0)
        send_z(3, 1)
        send_y(4, 0)
        send_y(4, 1)
        hand_over(4, half(2, True))

    loads[2].wait()
    grad_peer(0)
    grad_peer(1)
    grad_own(0)
    phase_one(0)
    grad_peer(2)
    grad_own(1)
    x_event_first()
    phase_one(1)
    grad_peer(3)
    grad_own(2)
    z_event(0)
    phase_one(2)
    grad_own(3)
    x_event_second()
    opposite_event()
    phase_one(3)
    pass_on("X1", 4, half(0, False), right)
    pass_on("X1", 5, half(0, False), left)
    first_y(0)
    first_z(0)
    first_y(1)
    first_z(1)
    y_event(0)
    first_y(2)
    first_z(2)
    z_event(1)
    z_event(2)
    first_x()
    first_y(3)
    first_z(3)
    second_y()
    z_event(3)
    loads[7].wait()
    loads[8].wait()
    arrived("CF", 6, 7)
    ctx_work(0)
    y_event(4)
    third_z()
    third_y()
    third_x()
    y_event(1)
    y_event(2)
    arrived("X1", 4, 5)
    hand_over(2, half(3, False))
    hand_over(3, half(1, False))
    y_event(3)
    share()
    arrived("CF", 0, 2, 8, 9, 1, 3, 10, 11)
    ctx_work(3)
    ctx_work(1)
    teach_most()
    share_on()
    arrived("CF", 4, 5, 12, 13)
    ctx_work(2)
    teach_rest()
    arrived("GC", *range(8))
    for zh in range(2):
        for yy in range(4):
            place(zh, yy)
    for copy in copies.values():
        copy.wait_send()


def communicate(student_ctx, out_grad, weight, teacher, teach_input, teach_ctx):
    anywhere = pl.BlockSpec(memory_space=pl.ANY)
    vmem = pltpu.VMEM
    return pl.pallas_call(
        kernel,
        out_shape=(
            pltpu.VMEM((TOKENS, D), BF16),
            pltpu.VMEM((TEACH, D), BF16),
            pltpu.VMEM((SHARD_ROWS, D), BF16),
        ),
        in_specs=[anywhere] * 6,
        out_specs=(pl.BlockSpec(memory_space=pltpu.VMEM),) * 3,
        scratch_shapes=[
            vmem((4, TOKENS, 384), BF16),
            vmem((TOKENS, D), BF16),
            vmem((SHARD_ROWS, D), F32),
            vmem((SHARD_ROWS, D), F32),
            vmem((TEACH, D), BF16),
            vmem((TEACH, D), BF16),
            vmem((2, 8, SHARD_ROWS, D), BF16),
            vmem((4, 384, HALF), F32),
            vmem((4, 384, HALF), F32),
            vmem((4, 384, HALF), F32),
            vmem((4, 3, 2, BLOCK, THIRD), BF16),
            vmem((4, 3, 2, BLOCK, THIRD), BF16),
            vmem((4, 3, SHARD_ROWS, LANES), BF16),
            vmem((4, 3, SHARD_ROWS, LANES), BF16),
            vmem((3, 384, THIRD), BF16),
            vmem((3, 384, THIRD), BF16),
            vmem((4, 2, BLOCK, THIRD), F32),
            vmem((3, 2, BLOCK, THIRD), F32),
            vmem((2, 2, SHARD_ROWS, LANES), F32),
            vmem((3, SHARD_ROWS, LANES), F32),
            vmem((4, 4, BLOCK, LANES), F32),
            vmem((3, 4, BLOCK, LANES), F32),
            vmem((2, 2, BLOCK, LANES), F32),
            vmem((3, BLOCK, LANES), F32),
            vmem((4, BLOCK, LANES), F32),
            vmem((3, BLOCK, LANES), F32),
            vmem((4, BLOCK, LANES), F32),
            vmem((3, BLOCK, LANES), F32),
            vmem((2, 4, 2, 3, BLOCK, LANES), BF16),
            vmem((TEACH, D), F32),
            pltpu.SemaphoreType.DMA((N_COPIES,)),
            pltpu.SemaphoreType.DMA((N_COPIES,)),
            pltpu.SemaphoreType.DMA((9,)),
        ],
        compiler_params=pltpu.CompilerParams(
            collective_id=0, has_side_effects=True, vmem_limit_bytes=54 * 2**20
        ),
        cost_estimate=pl.CostEstimate(
            flops=2 * D * D * (2 * TOKENS + TEACH), bytes_accessed=22 * 2**20, transcendentals=0
        ),
        name="exchange",
    )(student_ctx, out_grad, weight, teacher, teach_input, teach_ctx)


def finish_kernel(
    ctx_grad, teacher_out, gradient, weight, moment_one, moment_two, teacher,
    ctx_grad_o, weight_o, moment_one_o, moment_two_o, teacher_o, teacher_out_o,
    w_v, one_v, two_v, t_v, wo_v, oneo_v, twoo_v, to_v, in_sem, out_sem,
):
    loads = [
        pltpu.make_async_copy(src, dst, in_sem.at[i])
        for i, (src, dst) in enumerate([(weight, w_v), (moment_one, one_v), (moment_two, two_v), (teacher, t_v)])
    ]
    for load in loads:
        load.start()
    stores = []

    def store(src, dst):
        copy = pltpu.make_async_copy(src, dst, out_sem.at[len(stores)])
        copy.start()
        stores.append(copy)

    for r in range(4):
        rows = pl.ds(r * (TOKENS // 4), TOKENS // 4)
        store(ctx_grad.at[rows], ctx_grad_o.at[rows])
    for r in range(2):
        rows = pl.ds(r * (TEACH // 2), TEACH // 2)
        store(teacher_out.at[rows], teacher_out_o.at[rows])
    for load in loads:
        load.wait()
    correct_one = 1.0 - beta_one**STEP
    correct_two = 1.0 - beta_two**STEP
    for r in range(4):
        rows = pl.ds(r * BLOCK, BLOCK)
        g, w = gradient[rows, :].astype(F32), w_v[rows, :]
        one = beta_one * one_v[rows, :] + (1.0 - beta_one) * g
        two = beta_two * two_v[rows, :] + (1.0 - beta_two) * g * g
        update = one / correct_one / (jnp.sqrt(two / correct_two) + adam_eps) + decay_rate * w
        wo_v[rows, :] = w - learn_rate * update
        oneo_v[rows, :] = one
        twoo_v[rows, :] = two
        to_v[rows, :] = momentum * t_v[rows, :] + (1.0 - momentum) * w
        for src, dst in ((wo_v, weight_o), (oneo_v, moment_one_o), (twoo_v, moment_two_o), (to_v, teacher_o)):
            store(src.at[rows], dst.at[rows])
    for copy in stores:
        copy.wait()


def finish(ctx_grad, teacher_out, gradient, weight, moment_one, moment_two, teacher):
    anywhere, near = pl.BlockSpec(memory_space=pl.ANY), pl.BlockSpec(memory_space=pltpu.VMEM)
    state = jax.ShapeDtypeStruct((SHARD_ROWS, D), F32)
    return pl.pallas_call(
        finish_kernel,
        out_shape=(
            jax.ShapeDtypeStruct((TOKENS, D), BF16), state, state, state, state,
            jax.ShapeDtypeStruct((TEACH, D), BF16),
        ),
        in_specs=[near] * 3 + [anywhere] * 4,
        out_specs=(anywhere,) * 6,
        scratch_shapes=[pltpu.VMEM((SHARD_ROWS, D), F32)] * 8
        + [pltpu.SemaphoreType.DMA((4,)), pltpu.SemaphoreType.DMA((22,))],
        compiler_params=pltpu.CompilerParams(vmem_limit_bytes=24 * 2**20),
        cost_estimate=pl.CostEstimate(flops=10 * SHARD_ROWS * D, bytes_accessed=16 * 2**20, transcendentals=0),
        name="finish",
    )(ctx_grad, teacher_out, gradient, weight, moment_one, moment_two, teacher)


def body(student_ctx, out_grad, weight, moment_one, moment_two, teacher, teach_input, teach_ctx):
    ctx_grad, teacher_out, gradient = communicate(
        student_ctx, out_grad, weight, teacher, teach_input, teach_ctx
    )
    return finish(ctx_grad, teacher_out, gradient, weight, moment_one, moment_two, teacher)


def solution(mesh):
    return jax.shard_map(
        body,
        mesh=mesh,
        in_specs=(
            P(("replica", "shard"), None),
            P(("replica", "shard"), None),
            P("shard", None),
            P("shard", None),
            P("shard", None),
            P("shard", None),
            P(("replica", "shard"), None),
            P(("replica", "shard"), None),
        ),
        out_specs=(
            P(("replica", "shard"), None),
            P("shard", None),
            P("shard", None),
            P("shard", None),
            P("shard", None),
            P(("replica", "shard"), None),
        ),
        check_vma=False,
    )
```

```python
import jax
import jax.numpy as jnp
from jax import lax
from jax.experimental import pallas as pl
from jax.experimental.pallas import tpu as pltpu
from jax.sharding import PartitionSpec as P

STEP = 100


beta_one = 0.9
beta_two = 0.999
adam_eps = 1e-08
learn_rate = 0.001
decay_rate = 0.04
momentum = 0.994

F32 = jnp.float32
BF16 = jnp.bfloat16
MESH = pl.DeviceIdType.MESH

D = 1536
HALF = D // 2
SHARD_ROWS = 192
PIECE_HALF = 96
BLOCK = 48
TOKENS = 1280
TEACH = 512

THIRD = 256
ORDER = (2, 1, 3, 0)
LANES = 128

sizes = dict(
    X1=6, X2=2, ZW=8, YW=8, CF=14, PAIR=4,
    Y1=12, Z1=12, XA=3, XB=3, ZB=3, YB=3, ZC=3, YC=3, XC=3, GA=7, GC=8,
)
first = {}
N_COPIES = 0
for name, size in sizes.items():
    first[name] = N_COPIES
    N_COPIES += size


def kernel(
    student_ctx, out_grad, weight, moment_one, moment_two, teacher, teach_input, teach_ctx,
    ctx_grad, teacher_out, gradient, w_v, one_v, two_v, next_v,
    ctx_v, og_v, t_v, tin_v, tctx_v,
    mats, g_peer, g_own, g_recv,
    y1_s, y1_r, z1_s, z1_r, xa_s, xa_r,
    xb_s, xb_r, zb_s, zb_r, yb_s, yb_r,
    zc_s, zc_r, yc_s, yc_r, xc_s, xc_r,
    rows_v, sum_v,
    send_sem, recv_sem, in_sem,
):
    replica, shard = lax.axis_index("replica"), lax.axis_index("shard")
    core, y = replica % 2, (replica // 2) % 4
    z_high = replica // 8
    z = z_high * 2 + shard % 2
    x, parity = shard // 2, shard % 2
    other = 1 - core
    h = y % 2

    def device(dx=0, dy=0, dz=0, flip=False):
        xx, yy, zz = (x + dx) % 4, (y + dy) % 4, (z + dz) % 4
        cc = other if flip else core
        return {"replica": ((zz // 2) * 4 + yy) * 2 + cc, "shard": xx * 2 + zz % 2}

    partners = [device(flip=True)]
    for step in (1, 2, 3):
        partners += [device(dx=step), device(dy=step), device(dz=step), device(dy=step, dz=2)]
    barrier = pltpu.get_barrier_semaphore()
    for partner in partners:
        pl.semaphore_signal(barrier, inc=1, device_id=partner, device_id_type=MESH)

    def ctx_columns_at(k):
        return pl.ds(pl.multiple_of(((x + ORDER[k]) % 4) * 384, 128), 384)

    pairs = [(weight, w_v), (teacher, t_v), (out_grad, og_v)]
    pairs += [(student_ctx.at[:, ctx_columns_at(k)], ctx_v.at[k]) for k in range(4)]
    pairs += [(teach_ctx, tctx_v), (teach_input, tin_v), (moment_one, one_v), (moment_two, two_v)]
    loads = [pltpu.make_async_copy(src, dst, in_sem.at[i]) for i, (src, dst) in enumerate(pairs)]
    for i in range(4):
        loads[i].start()

    copies = {}

    def send(name, i, src, dst, target):
        copies[name, i] = pltpu.make_async_remote_copy(
            src_ref=src, dst_ref=dst,
            send_sem=send_sem.at[first[name] + i], recv_sem=recv_sem.at[first[name] + i],
            device_id=target, device_id_type=MESH,
        )
        copies[name, i].start()

    def arrived(name, *ids):
        for i in ids:
            copies[name, i].wait_recv()

    loads[0].wait()
    loads[1].wait()
    for r in range(0, SHARD_ROWS, BLOCK):
        rows = pl.ds(r, BLOCK)
        w = w_v[rows, :]
        mats[0, shard, rows, :] = w.astype(BF16)
        blend = momentum * t_v[rows, :] + (1.0 - momentum) * w
        next_v[rows, :] = blend
        mats[1, shard, rows, :] = blend.astype(BF16)

    for i in range(4, 11):
        loads[i].start()
    pl.semaphore_wait(barrier, len(partners))

    right, left, up, down = device(dx=1), device(dx=3), device(dz=1), device(dz=3)
    north, south, twin = device(dy=1), device(dy=3), device(flip=True)
    offsets = (0, 3, 1, 2)

    def piece(dx, start, size, flipped):
        index = ((x + dx) % 4) * 2 + ((1 - parity) if flipped else parity)
        return mats.at[core, index, pl.ds(pl.multiple_of(start, 16), size)]

    def half(dx, near, flipped=False):
        return piece(dx, (h if near else 1 - h) * 96, 96, flipped)

    def quarter(dx, q, flipped=False):
        return piece(dx, h * 96 + q * 48, 48, flipped)

    def pass_on(name, i, ref, target):
        send(name, i, ref, ref, target)

    def send_z(j, q):
        ref = quarter(offsets[j], q) if j else piece(0, q * 96, 96, False)
        pass_on("ZW", 2 * j + q, ref, up if q == 0 else down)

    def send_y(j, q):
        ref = quarter(offsets[j], q, True) if j < 4 else quarter(2, q)
        pass_on("YW", 2 * j - 2 + q, ref, north if q == 0 else south)

    def hand_over(slot, ref):
        pass_on("CF", slot, ref, twin)

    def z_event(j):
        arrived("ZW", 2 * j, 2 * j + 1)
        hand_over(6 + 2 * j, half(offsets[j], True, True))
        if j == 0:
            hand_over(7, half(0, False, True))
        else:
            send_y(j, 0)
            send_y(j, 1)

    def y_event(j):
        arrived("YW", 2 * j - 2, 2 * j - 1)
        if j < 4:
            hand_over(7 + 2 * j, half(offsets[j], False, True))
        else:
            hand_over(5, half(2, False))

    pass_on("X1", 0, quarter(0, 0), right)
    pass_on("X1", 1, quarter(0, 1), left)
    pass_on("X1", 2, quarter(0, 1), right)
    pass_on("X1", 3, quarter(0, 0), left)
    send_z(0, 0)
    send_z(0, 1)

    def grad_part(k, side):
        return lax.dot_general(
            ctx_v[k], og_v[:, pl.ds(pl.multiple_of(side * HALF, 128), HALF)],
            (((0,), (0,)), ((), ())), preferred_element_type=F32,
        )

    def grad_peer(k):
        loads[3 + k].wait()
        g_peer[k] = grad_part(k, other)
        send("PAIR", k, g_peer.at[k], g_recv.at[k], twin)

    def grad_own(k):
        g_own[k] = grad_part(k, core)

    def both(k, row, n_rows, column, n_columns):
        at = (k, pl.ds(pl.multiple_of(row, 16), n_rows), pl.ds(pl.multiple_of(column, 128), n_columns))
        return g_own[at] + g_recv[at]

    def phase_one(k):
        arrived("PAIR", k)
        if k < 3:
            xa_s[k] = both(k, 0, 384, THIRD, THIRD).astype(BF16)
            send("XA", k, xa_s.at[k], xa_r.at[k], device(dx=ORDER[k]))
        for j in range(3):
            yy = (y + 1 + j) % 4
            for par in (0, 1):
                y1_s[k, j, par] = both(k, par * SHARD_ROWS + yy * BLOCK, BLOCK, 0, THIRD).astype(BF16)
            send("Y1", 3 * k + j, y1_s.at[k, j], y1_r.at[k, j], device(dy=1 + j))
            zz = (z + 1 + j) % 4
            z1_s[k, j] = both(
                k, (zz % 2) * SHARD_ROWS, SHARD_ROWS, 2 * THIRD + (zz // 2) * LANES, LANES
            ).astype(BF16)
            send("Z1", 3 * k + j, z1_s.at[k, j], z1_r.at[k, j], device(dz=1 + j))

    def first_y(k):
        arrived("Y1", 3 * k, 3 * k + 1, 3 * k + 2)
        for par in (0, 1):
            total = both(k, par * SHARD_ROWS + y * BLOCK, BLOCK, 0, THIRD)
            for j in range(3):
                total = total + y1_r[k, j, par].astype(F32)
            xb_s[k, par] = total
        if k < 3:
            send("XB", k, xb_s.at[k], xb_r.at[k], device(dx=ORDER[k]))

    def first_z(k):
        arrived("Z1", 3 * k, 3 * k + 1, 3 * k + 2)
        for yy in range(4):
            rows = pl.ds(yy * BLOCK, BLOCK)
            total = both(k, parity * SHARD_ROWS + yy * BLOCK, BLOCK, 2 * THIRD + z_high * LANES, LANES)
            for j in range(3):
                total = total + z1_r[k, j, rows, :].astype(F32)
            yb_s[yy, k] = total

    def first_x():
        arrived("XA", 0, 1, 2)
        for par in (0, 1):
            for zh in (0, 1):
                for q in range(4):
                    rows = pl.ds(par * SHARD_ROWS + q * BLOCK, BLOCK)
                    lanes = pl.ds(zh * LANES, LANES)
                    total = both(3, par * SHARD_ROWS + q * BLOCK, BLOCK, THIRD + zh * LANES, LANES)
                    for k in range(3):
                        total = total + xa_r[k, rows, lanes].astype(F32)
                    zb_s[par, zh, q * BLOCK:(q + 1) * BLOCK, :] = total
        for j in range(3):
            zz = (z + 1 + j) % 4
            send("ZB", j, zb_s.at[zz % 2, zz // 2], zb_r.at[j], device(dz=1 + j))

    def second_y():
        for j in range(3):
            send("YB", j, yb_s.at[(y + 1 + j) % 4], yb_r.at[j], device(dy=1 + j))

    def third_z():
        arrived("XB", 0, 1, 2)
        for par in (0, 1):
            for zh in (0, 1):
                lanes = pl.ds(zh * LANES, LANES)
                zc_s[par, zh] = (
                    xb_s[3, par, :, lanes] + xb_r[0, par, :, lanes] + xb_r[1, par, :, lanes] + xb_r[2, par, :, lanes]
                )
        for j in range(3):
            zz = (z + 1 + j) % 4
            send("ZC", j, zc_s.at[zz % 2, zz // 2], zc_r.at[j], device(dz=1 + j))

    def third_y():
        arrived("ZB", 0, 1, 2)
        for yy in range(4):
            rows = pl.ds(yy * BLOCK, BLOCK)
            yc_s[yy] = zb_s[parity, z_high, rows, :] + zb_r[0, rows, :] + zb_r[1, rows, :] + zb_r[2, rows, :]
        for j in range(3):
            send("YC", j, yc_s.at[(y + 1 + j) % 4], yc_r.at[j], device(dy=1 + j))

    def third_x():
        arrived("YB", 0, 1, 2)
        for k in range(4):
            xc_s[k] = yb_s[y, k] + yb_r[0, k] + yb_r[1, k] + yb_r[2, k]
        for k in range(3):
            send("XC", k, xc_s.at[k], xc_r.at[k], device(dx=ORDER[k]))

    steps = [(0, 1), (0, 3), (0, 2), (2, 0), (2, 1), (2, 3), (2, 2)]

    def share():
        arrived("ZC", 0, 1, 2)
        rows_v[z_high, y, core, 0] = (
            zc_s[parity, z_high] + zc_r[0] + zc_r[1] + zc_r[2]
        ).astype(BF16)
        arrived("YC", 0, 1, 2)
        rows_v[z_high, y, core, 1] = (yc_s[y] + yc_r[0] + yc_r[1] + yc_r[2]).astype(BF16)
        arrived("XC", 0, 1, 2)
        rows_v[z_high, y, core, 2] = (xc_s[3] + xc_r[0] + xc_r[1] + xc_r[2]).astype(BF16)
        own = rows_v.at[z_high, y, core]
        for i, (dz, dy) in enumerate(steps):
            send("GA", i, own, own, device(dy=dy, dz=dz))
        send("GC", 7, own, own, twin)

    def share_on():
        for i, (dz, dy) in enumerate(steps):
            arrived("GA", i)
            got = rows_v.at[(z_high + dz // 2) % 2, (y + 4 - dy) % 4, core]
            send("GC", i, got, got, twin)

    def place(zh, yy):
        for cc in range(2):
            for third in range(3):
                start = cc * HALF + third * THIRD + zh * LANES
                gradient[yy * BLOCK:(yy + 1) * BLOCK, start:start + LANES] = rows_v[zh, yy, cc, third]

    def columns_of(dx):
        return pl.ds(pl.multiple_of(((x + dx) % 4) * 384, 128), 384)

    def pieces_of(m, dx):
        return mats[m, pl.ds(((x + dx) % 4) * 2, 2)].reshape(2 * SHARD_ROWS, D)

    def ctx_work(dx):
        ctx_grad[:, columns_of(dx)] = lax.dot_general(
            og_v[...], pieces_of(0, dx), (((1,), (1,)), ((), ())), preferred_element_type=F32
        ).astype(BF16)

    def teach_part(dx, at):
        return jnp.dot(
            tctx_v[:, columns_of(dx)], mats[1, pl.ds(((x + dx) % 4) * 2, 2), :, at].reshape(2 * SHARD_ROWS, HALF),
            preferred_element_type=F32,
        )

    def teach_first():
        def step(n, _):
            at = pl.ds(pl.multiple_of(n * HALF, 128), HALF)
            sum_v[:, at] = teach_part(0, at)
            return 0

        lax.fori_loop(0, 2, step, 0)

    def teach_most():
        def step(n, _):
            at = pl.ds(pl.multiple_of(n * HALF, 128), HALF)
            sum_v[:, at] = sum_v[:, at] + (teach_part(3, at) + teach_part(1, at))
            return 0

        lax.fori_loop(0, 2, step, 0)

    def teach_rest():
        def step(n, _):
            at = pl.ds(pl.multiple_of(n * HALF, 128), HALF)
            teacher_out[:, at] = (tin_v[:, at].astype(F32) + (sum_v[:, at] + teach_part(2, at))).astype(BF16)
            return 0

        lax.fori_loop(0, 2, step, 0)

    def x_event_first():
        arrived("X1", 0, 1)
        pass_on("X2", 0, quarter(3, 0), right)
        pass_on("X2", 1, quarter(1, 1), left)
        send_z(1, 0)
        send_z(2, 1)

    def x_event_second():
        arrived("X1", 2, 3)
        send_z(1, 1)
        send_z(2, 0)
        hand_over(0, half(3, True))
        hand_over(1, half(1, True))

    def opposite_event():
        arrived("X2", 0, 1)
        send_z(3, 0)
        send_z(3, 1)
        send_y(4, 0)
        send_y(4, 1)
        hand_over(4, half(2, True))

    loads[2].wait()
    grad_peer(0)
    grad_peer(1)
    grad_own(0)
    phase_one(0)
    grad_peer(2)
    grad_own(1)
    x_event_first()
    phase_one(1)
    grad_peer(3)
    grad_own(2)
    z_event(0)
    phase_one(2)
    grad_own(3)
    x_event_second()
    opposite_event()
    phase_one(3)
    pass_on("X1", 4, half(0, False), right)
    pass_on("X1", 5, half(0, False), left)
    first_y(0)
    first_z(0)
    first_y(1)
    first_z(1)
    first_y(2)
    first_z(2)
    z_event(1)
    z_event(2)
    first_x()
    first_y(3)
    first_z(3)
    second_y()
    z_event(3)
    for i in range(7, 11):
        loads[i].wait()
    arrived("CF", 6, 7)
    ctx_work(0)
    teach_first()
    y_event(4)
    third_z()
    third_y()
    third_x()
    y_event(1)
    y_event(2)
    arrived("X1", 4, 5)
    hand_over(2, half(3, False))
    hand_over(3, half(1, False))
    y_event(3)
    share()
    arrived("CF", 0, 2, 8, 9, 1, 3, 10, 11)
    ctx_work(3)
    ctx_work(1)
    teach_most()
    share_on()
    arrived("CF", 4, 5, 12, 13)
    ctx_work(2)
    teach_rest()
    arrived("GC", *range(8))
    for zh in range(2):
        for yy in range(4):
            place(zh, yy)
    for copy in copies.values():
        copy.wait_send()


def communicate(*operands):
    anywhere = pl.BlockSpec(memory_space=pl.ANY)
    vmem = pltpu.VMEM
    return pl.pallas_call(
        kernel,
        out_shape=(
            pltpu.VMEM((TOKENS, D), BF16),
            pltpu.VMEM((TEACH, D), BF16),
            pltpu.VMEM((SHARD_ROWS, D), BF16),
        )
        + (pltpu.VMEM((SHARD_ROWS, D), F32),) * 4,
        in_specs=[anywhere] * 8,
        out_specs=(pl.BlockSpec(memory_space=pltpu.VMEM),) * 7,
        scratch_shapes=[
            vmem((4, TOKENS, 384), BF16),
            vmem((TOKENS, D), BF16),
            vmem((SHARD_ROWS, D), F32),
            vmem((TEACH, D), BF16),
            vmem((TEACH, D), BF16),
            vmem((2, 8, SHARD_ROWS, D), BF16),
            vmem((4, 384, HALF), F32),
            vmem((4, 384, HALF), F32),
            vmem((4, 384, HALF), F32),
            vmem((4, 3, 2, BLOCK, THIRD), BF16),
            vmem((4, 3, 2, BLOCK, THIRD), BF16),
            vmem((4, 3, SHARD_ROWS, LANES), BF16),
            vmem((4, 3, SHARD_ROWS, LANES), BF16),
            vmem((3, 384, THIRD), BF16),
            vmem((3, 384, THIRD), BF16),
            vmem((4, 2, BLOCK, THIRD), F32),
            vmem((3, 2, BLOCK, THIRD), F32),
            vmem((2, 2, SHARD_ROWS, LANES), F32),
            vmem((3, SHARD_ROWS, LANES), F32),
            vmem((4, 4, BLOCK, LANES), F32),
            vmem((3, 4, BLOCK, LANES), F32),
            vmem((2, 2, BLOCK, LANES), F32),
            vmem((3, BLOCK, LANES), F32),
            vmem((4, BLOCK, LANES), F32),
            vmem((3, BLOCK, LANES), F32),
            vmem((4, BLOCK, LANES), F32),
            vmem((3, BLOCK, LANES), F32),
            vmem((2, 4, 2, 3, BLOCK, LANES), BF16),
            vmem((TEACH, D), F32),
            pltpu.SemaphoreType.DMA((N_COPIES,)),
            pltpu.SemaphoreType.DMA((N_COPIES,)),
            pltpu.SemaphoreType.DMA((11,)),
        ],
        compiler_params=pltpu.CompilerParams(
            collective_id=0, has_side_effects=True, vmem_limit_bytes=50 * 2**20
        ),
        cost_estimate=pl.CostEstimate(
            flops=2 * D * D * (2 * TOKENS + TEACH), bytes_accessed=22 * 2**20, transcendentals=0
        ),
        name="exchange",
    )(*operands)


def finish_kernel(
    ctx_grad, teacher_out, gradient, weight, moment_one, moment_two, teacher_next,
    ctx_grad_o, weight_o, moment_one_o, moment_two_o, teacher_o, teacher_out_o,
    wo_v, oneo_v, twoo_v, out_sem,
):
    stores = []

    def store(src, dst):
        copy = pltpu.make_async_copy(src, dst, out_sem.at[len(stores)])
        copy.start()
        stores.append(copy)

    store(teacher_next, teacher_o)
    for r in range(4):
        rows = pl.ds(r * (TOKENS // 4), TOKENS // 4)
        store(ctx_grad.at[rows], ctx_grad_o.at[rows])
    for r in range(2):
        rows = pl.ds(r * (TEACH // 2), TEACH // 2)
        store(teacher_out.at[rows], teacher_out_o.at[rows])
    correct_one = 1.0 - beta_one**STEP
    correct_two = 1.0 - beta_two**STEP
    for r in range(4):
        rows = pl.ds(r * BLOCK, BLOCK)
        g, w = gradient[rows, :].astype(F32), weight[rows, :]
        one = beta_one * moment_one[rows, :] + (1.0 - beta_one) * g
        two = beta_two * moment_two[rows, :] + (1.0 - beta_two) * g * g
        update = one / correct_one / (jnp.sqrt(two / correct_two) + adam_eps) + decay_rate * w
        wo_v[rows, :] = w - learn_rate * update
        oneo_v[rows, :] = one
        twoo_v[rows, :] = two
        for src, dst in ((wo_v, weight_o), (oneo_v, moment_one_o), (twoo_v, moment_two_o)):
            store(src.at[rows], dst.at[rows])
    for copy in stores:
        copy.wait()


def finish(*operands):
    anywhere, near = pl.BlockSpec(memory_space=pl.ANY), pl.BlockSpec(memory_space=pltpu.VMEM)
    state = jax.ShapeDtypeStruct((SHARD_ROWS, D), F32)
    return pl.pallas_call(
        finish_kernel,
        out_shape=(
            jax.ShapeDtypeStruct((TOKENS, D), BF16), state, state, state, state,
            jax.ShapeDtypeStruct((TEACH, D), BF16),
        ),
        in_specs=[near] * 7,
        out_specs=(anywhere,) * 6,
        scratch_shapes=[pltpu.VMEM((SHARD_ROWS, D), F32)] * 3 + [pltpu.SemaphoreType.DMA((19,))],
        compiler_params=pltpu.CompilerParams(vmem_limit_bytes=24 * 2**20),
        cost_estimate=pl.CostEstimate(flops=10 * SHARD_ROWS * D, bytes_accessed=12 * 2**20, transcendentals=0),
        name="finish",
    )(*operands)


def body(student_ctx, out_grad, weight, moment_one, moment_two, teacher, teach_input, teach_ctx):
    results = communicate(
        student_ctx, out_grad, weight, moment_one, moment_two, teacher, teach_input, teach_ctx
    )
    return finish(*results)


def solution(mesh):
    return jax.shard_map(
        body,
        mesh=mesh,
        in_specs=(
            P(("replica", "shard"), None),
            P(("replica", "shard"), None),
            P("shard", None),
            P("shard", None),
            P("shard", None),
            P("shard", None),
            P(("replica", "shard"), None),
            P(("replica", "shard"), None),
        ),
        out_specs=(
            P(("replica", "shard"), None),
            P("shard", None),
            P("shard", None),
            P("shard", None),
            P("shard", None),
            P(("replica", "shard"), None),
        ),
        check_vma=False,
    )
```

```python
import jax
import jax.numpy as jnp
from jax import lax
from jax.experimental import pallas as pl
from jax.experimental.pallas import tpu as pltpu
from jax.sharding import PartitionSpec as P

STEP = 100


beta_one = 0.9
beta_two = 0.999
adam_eps = 1e-08
learn_rate = 0.001
decay_rate = 0.04
momentum = 0.994

F32 = jnp.float32
BF16 = jnp.bfloat16
MESH = pl.DeviceIdType.MESH

D = 1536
HALF = D // 2
SHARD_ROWS = 192
PIECE_HALF = 96
BLOCK = 48
TOKENS = 1280
TEACH = 512

THIRD = 256
ORDER = (2, 1, 3, 0)
LANES = 128

sizes = dict(
    X1=6, X2=2, ZW=8, YW=8, CF=14, PAIR=4,
    Y1=12, Z1=12, XA=3, XB=3, ZB=3, YB=3, ZC=3, YC=3, XC=3, GA=7, GC=8,
)
first = {}
N_COPIES = 0
for name, size in sizes.items():
    first[name] = N_COPIES
    N_COPIES += size


def kernel(
    student_ctx, out_grad, weight, moment_one, moment_two, teacher, teach_input, teach_ctx,
    ctx_grad, teacher_out, gradient, w_v, one_v, two_v, next_v,
    ctx_v, og_v, t_v, tin_v, tctx_v,
    mats, g_peer, g_own, g_recv,
    y1_s, y1_r, z1_s, z1_r, xa_s, xa_r,
    xb_s, xb_r, zb_s, zb_r, yb_s, yb_r,
    zc_s, zc_r, yc_s, yc_r, xc_s, xc_r,
    rows_v, sum_v,
    send_sem, recv_sem, in_sem,
):
    replica, shard = lax.axis_index("replica"), lax.axis_index("shard")
    core, y = replica % 2, (replica // 2) % 4
    z_high = replica // 8
    z = z_high * 2 + shard % 2
    x, parity = shard // 2, shard % 2
    other = 1 - core
    h = y % 2

    def device(dx=0, dy=0, dz=0, flip=False):
        xx, yy, zz = (x + dx) % 4, (y + dy) % 4, (z + dz) % 4
        cc = other if flip else core
        return {"replica": ((zz // 2) * 4 + yy) * 2 + cc, "shard": xx * 2 + zz % 2}

    partners = [device(flip=True)]
    for step in (1, 2, 3):
        partners += [device(dx=step), device(dy=step), device(dz=step), device(dy=step, dz=2)]
    barrier = pltpu.get_barrier_semaphore()
    for partner in partners:
        pl.semaphore_signal(barrier, inc=1, device_id=partner, device_id_type=MESH)

    def ctx_columns_at(k):
        return pl.ds(pl.multiple_of(((x + ORDER[k]) % 4) * 384, 128), 384)

    pairs = [(weight, w_v), (teacher, t_v), (out_grad, og_v)]
    pairs += [(student_ctx.at[:, ctx_columns_at(k)], ctx_v.at[k]) for k in range(4)]
    pairs += [(teach_ctx, tctx_v), (teach_input, tin_v), (moment_one, one_v), (moment_two, two_v)]
    loads = [pltpu.make_async_copy(src, dst, in_sem.at[i]) for i, (src, dst) in enumerate(pairs)]
    for i in range(4):
        loads[i].start()

    copies = {}

    def send(name, i, src, dst, target):
        copies[name, i] = pltpu.make_async_remote_copy(
            src_ref=src, dst_ref=dst,
            send_sem=send_sem.at[first[name] + i], recv_sem=recv_sem.at[first[name] + i],
            device_id=target, device_id_type=MESH,
        )
        copies[name, i].start()

    def arrived(name, *ids):
        for i in ids:
            copies[name, i].wait_recv()

    loads[0].wait()
    loads[1].wait()
    for r in range(0, SHARD_ROWS, BLOCK):
        rows = pl.ds(r, BLOCK)
        w = w_v[rows, :]
        mats[0, shard, rows, :] = w.astype(BF16)
        blend = momentum * t_v[rows, :] + (1.0 - momentum) * w
        next_v[rows, :] = blend
        mats[1, shard, rows, :] = blend.astype(BF16)

    for i in range(4, 11):
        loads[i].start()
    pl.semaphore_wait(barrier, len(partners))

    right, left, up, down = device(dx=1), device(dx=3), device(dz=1), device(dz=3)
    north, south, twin = device(dy=1), device(dy=3), device(flip=True)
    offsets = (0, 3, 1, 2)

    def piece(dx, start, size, flipped):
        index = ((x + dx) % 4) * 2 + ((1 - parity) if flipped else parity)
        return mats.at[core, index, pl.ds(pl.multiple_of(start, 16), size)]

    def half(dx, near, flipped=False):
        return piece(dx, (h if near else 1 - h) * 96, 96, flipped)

    def quarter(dx, q, flipped=False):
        return piece(dx, h * 96 + q * 48, 48, flipped)

    def pass_on(name, i, ref, target):
        send(name, i, ref, ref, target)

    def send_z(j, q):
        ref = quarter(offsets[j], q) if j else piece(0, q * 96, 96, False)
        pass_on("ZW", 2 * j + q, ref, up if q == 0 else down)

    def send_y(j, q):
        ref = quarter(offsets[j], q, True) if j < 4 else quarter(2, q)
        pass_on("YW", 2 * j - 2 + q, ref, north if q == 0 else south)

    def hand_over(slot, ref):
        pass_on("CF", slot, ref, twin)

    def z_event(j):
        arrived("ZW", 2 * j, 2 * j + 1)
        hand_over(6 + 2 * j, half(offsets[j], True, True))
        if j == 0:
            hand_over(7, half(0, False, True))
        else:
            send_y(j, 0)
            send_y(j, 1)

    def y_event(j):
        arrived("YW", 2 * j - 2, 2 * j - 1)
        if j < 4:
            hand_over(7 + 2 * j, half(offsets[j], False, True))
        else:
            hand_over(5, half(2, False))

    pass_on("X1", 0, quarter(0, 0), right)
    pass_on("X1", 1, quarter(0, 1), left)
    pass_on("X1", 2, quarter(0, 1), right)
    pass_on("X1", 3, quarter(0, 0), left)
    send_z(0, 0)
    send_z(0, 1)

    def grad_part(k, side):
        return lax.dot_general(
            ctx_v[k], og_v[:, pl.ds(pl.multiple_of(side * HALF, 128), HALF)],
            (((0,), (0,)), ((), ())), preferred_element_type=F32,
        )

    def grad_peer(k):
        loads[3 + k].wait()
        g_peer[k] = grad_part(k, other)
        send("PAIR", k, g_peer.at[k], g_recv.at[k], twin)

    def grad_own(k):
        g_own[k] = grad_part(k, core)

    def both(k, row, n_rows, column, n_columns):
        at = (k, pl.ds(pl.multiple_of(row, 16), n_rows), pl.ds(pl.multiple_of(column, 128), n_columns))
        return g_own[at] + g_recv[at]

    def phase_one(k):
        arrived("PAIR", k)
        if k < 3:
            xa_s[k] = both(k, 0, 384, THIRD, THIRD).astype(BF16)
            send("XA", k, xa_s.at[k], xa_r.at[k], device(dx=ORDER[k]))
        for j in range(3):
            yy = (y + 1 + j) % 4
            for par in (0, 1):
                y1_s[k, j, par] = both(k, par * SHARD_ROWS + yy * BLOCK, BLOCK, 0, THIRD).astype(BF16)
            send("Y1", 3 * k + j, y1_s.at[k, j], y1_r.at[k, j], device(dy=1 + j))
            zz = (z + 1 + j) % 4
            z1_s[k, j] = both(
                k, (zz % 2) * SHARD_ROWS, SHARD_ROWS, 2 * THIRD + (zz // 2) * LANES, LANES
            ).astype(BF16)
            send("Z1", 3 * k + j, z1_s.at[k, j], z1_r.at[k, j], device(dz=1 + j))

    def first_y(k):
        arrived("Y1", 3 * k, 3 * k + 1, 3 * k + 2)
        for par in (0, 1):
            total = both(k, par * SHARD_ROWS + y * BLOCK, BLOCK, 0, THIRD)
            for j in range(3):
                total = total + y1_r[k, j, par].astype(F32)
            xb_s[k, par] = total
        if k < 3:
            send("XB", k, xb_s.at[k], xb_r.at[k], device(dx=ORDER[k]))

    def first_z(k):
        arrived("Z1", 3 * k, 3 * k + 1, 3 * k + 2)
        for yy in range(4):
            rows = pl.ds(yy * BLOCK, BLOCK)
            total = both(k, parity * SHARD_ROWS + yy * BLOCK, BLOCK, 2 * THIRD + z_high * LANES, LANES)
            for j in range(3):
                total = total + z1_r[k, j, rows, :].astype(F32)
            yb_s[yy, k] = total

    def first_x():
        arrived("XA", 0, 1, 2)
        for par in (0, 1):
            for zh in (0, 1):
                for q in range(4):
                    rows = pl.ds(par * SHARD_ROWS + q * BLOCK, BLOCK)
                    lanes = pl.ds(zh * LANES, LANES)
                    total = both(3, par * SHARD_ROWS + q * BLOCK, BLOCK, THIRD + zh * LANES, LANES)
                    for k in range(3):
                        total = total + xa_r[k, rows, lanes].astype(F32)
                    zb_s[par, zh, q * BLOCK:(q + 1) * BLOCK, :] = total
        for j in range(3):
            zz = (z + 1 + j) % 4
            send("ZB", j, zb_s.at[zz % 2, zz // 2], zb_r.at[j], device(dz=1 + j))

    def second_y():
        for j in range(3):
            send("YB", j, yb_s.at[(y + 1 + j) % 4], yb_r.at[j], device(dy=1 + j))

    def third_z():
        arrived("XB", 0, 1, 2)
        for par in (0, 1):
            for zh in (0, 1):
                lanes = pl.ds(zh * LANES, LANES)
                zc_s[par, zh] = (
                    xb_s[3, par, :, lanes] + xb_r[0, par, :, lanes] + xb_r[1, par, :, lanes] + xb_r[2, par, :, lanes]
                )
        for j in range(3):
            zz = (z + 1 + j) % 4
            send("ZC", j, zc_s.at[zz % 2, zz // 2], zc_r.at[j], device(dz=1 + j))

    def third_y():
        arrived("ZB", 0, 1, 2)
        for yy in range(4):
            rows = pl.ds(yy * BLOCK, BLOCK)
            yc_s[yy] = zb_s[parity, z_high, rows, :] + zb_r[0, rows, :] + zb_r[1, rows, :] + zb_r[2, rows, :]
        for j in range(3):
            send("YC", j, yc_s.at[(y + 1 + j) % 4], yc_r.at[j], device(dy=1 + j))

    def third_x():
        arrived("YB", 0, 1, 2)
        for k in range(4):
            xc_s[k] = yb_s[y, k] + yb_r[0, k] + yb_r[1, k] + yb_r[2, k]
        for k in range(3):
            send("XC", k, xc_s.at[k], xc_r.at[k], device(dx=ORDER[k]))

    steps = [(0, 1), (0, 3), (0, 2), (2, 0), (2, 1), (2, 3), (2, 2)]

    def share():
        arrived("ZC", 0, 1, 2)
        rows_v[z_high, y, core, 0] = (
            zc_s[parity, z_high] + zc_r[0] + zc_r[1] + zc_r[2]
        ).astype(BF16)
        arrived("YC", 0, 1, 2)
        rows_v[z_high, y, core, 1] = (yc_s[y] + yc_r[0] + yc_r[1] + yc_r[2]).astype(BF16)
        arrived("XC", 0, 1, 2)
        rows_v[z_high, y, core, 2] = (xc_s[3] + xc_r[0] + xc_r[1] + xc_r[2]).astype(BF16)
        own = rows_v.at[z_high, y, core]
        for i, (dz, dy) in enumerate(steps):
            send("GA", i, own, own, device(dy=dy, dz=dz))
        send("GC", 7, own, own, twin)

    def share_on():
        for i, (dz, dy) in enumerate(steps):
            arrived("GA", i)
            got = rows_v.at[(z_high + dz // 2) % 2, (y + 4 - dy) % 4, core]
            send("GC", i, got, got, twin)

    def place(zh, yy):
        for cc in range(2):
            for third in range(3):
                start = cc * HALF + third * THIRD + zh * LANES
                gradient[yy * BLOCK:(yy + 1) * BLOCK, start:start + LANES] = rows_v[zh, yy, cc, third]

    def columns_of(dx):
        return pl.ds(pl.multiple_of(((x + dx) % 4) * 384, 128), 384)

    def pieces_of(m, dx):
        return mats[m, pl.ds(((x + dx) % 4) * 2, 2)].reshape(2 * SHARD_ROWS, D)

    def ctx_work(dx):
        ctx_grad[:, columns_of(dx)] = lax.dot_general(
            og_v[...], pieces_of(0, dx), (((1,), (1,)), ((), ())), preferred_element_type=F32
        ).astype(BF16)

    def teach_part(dx, at):
        return jnp.dot(
            tctx_v[:, columns_of(dx)], mats[1, pl.ds(((x + dx) % 4) * 2, 2), :, at].reshape(2 * SHARD_ROWS, HALF),
            preferred_element_type=F32,
        )

    def teach_first():
        def step(n, _):
            at = pl.ds(pl.multiple_of(n * HALF, 128), HALF)
            sum_v[:, at] = teach_part(0, at)
            return 0

        lax.fori_loop(0, 2, step, 0)

    def teach_most():
        def step(n, _):
            at = pl.ds(pl.multiple_of(n * HALF, 128), HALF)
            sum_v[:, at] = sum_v[:, at] + (teach_part(3, at) + teach_part(1, at))
            return 0

        lax.fori_loop(0, 2, step, 0)

    def teach_rest():
        def step(n, _):
            at = pl.ds(pl.multiple_of(n * HALF, 128), HALF)
            teacher_out[:, at] = (tin_v[:, at].astype(F32) + (sum_v[:, at] + teach_part(2, at))).astype(BF16)
            return 0

        lax.fori_loop(0, 2, step, 0)

    def x_event_first():
        arrived("X1", 0, 1)
        pass_on("X2", 0, quarter(3, 0), right)
        pass_on("X2", 1, quarter(1, 1), left)
        send_z(1, 0)
        send_z(2, 1)

    def x_event_second():
        arrived("X1", 2, 3)
        send_z(1, 1)
        send_z(2, 0)
        hand_over(0, half(3, True))
        hand_over(1, half(1, True))

    def opposite_event():
        arrived("X2", 0, 1)
        send_z(3, 0)
        send_z(3, 1)
        send_y(4, 0)
        send_y(4, 1)
        hand_over(4, half(2, True))

    loads[2].wait()
    grad_peer(0)
    grad_peer(1)
    grad_own(0)
    phase_one(0)
    grad_peer(2)
    grad_own(1)
    x_event_first()
    phase_one(1)
    grad_peer(3)
    grad_own(2)
    z_event(0)
    phase_one(2)
    grad_own(3)
    x_event_second()
    phase_one(3)
    opposite_event()
    pass_on("X1", 4, half(0, False), right)
    pass_on("X1", 5, half(0, False), left)
    first_y(0)
    first_z(0)
    first_y(1)
    first_z(1)
    first_y(2)
    first_z(2)
    z_event(1)
    z_event(2)
    first_x()
    first_y(3)
    first_z(3)
    second_y()
    z_event(3)
    for i in range(7, 11):
        loads[i].wait()
    arrived("CF", 6, 7)
    ctx_work(0)
    teach_first()
    y_event(4)
    third_z()
    third_y()
    third_x()
    y_event(1)
    y_event(2)
    arrived("X1", 4, 5)
    hand_over(2, half(3, False))
    hand_over(3, half(1, False))
    y_event(3)
    share()
    arrived("CF", 0, 2, 8, 9, 1, 3, 10, 11)
    ctx_work(3)
    ctx_work(1)
    teach_most()
    share_on()
    arrived("CF", 4, 5, 12, 13)
    ctx_work(2)
    teach_rest()
    arrived("GC", *range(8))
    for zh in range(2):
        for yy in range(4):
            place(zh, yy)
    for copy in copies.values():
        copy.wait_send()


def communicate(*operands):
    anywhere = pl.BlockSpec(memory_space=pl.ANY)
    vmem = pltpu.VMEM
    return pl.pallas_call(
        kernel,
        out_shape=(
            pltpu.VMEM((TOKENS, D), BF16),
            pltpu.VMEM((TEACH, D), BF16),
            pltpu.VMEM((SHARD_ROWS, D), BF16),
        )
        + (pltpu.VMEM((SHARD_ROWS, D), F32),) * 4,
        in_specs=[anywhere] * 8,
        out_specs=(pl.BlockSpec(memory_space=pltpu.VMEM),) * 7,
        scratch_shapes=[
            vmem((4, TOKENS, 384), BF16),
            vmem((TOKENS, D), BF16),
            vmem((SHARD_ROWS, D), F32),
            vmem((TEACH, D), BF16),
            vmem((TEACH, D), BF16),
            vmem((2, 8, SHARD_ROWS, D), BF16),
            vmem((4, 384, HALF), F32),
            vmem((4, 384, HALF), F32),
            vmem((4, 384, HALF), F32),
            vmem((4, 3, 2, BLOCK, THIRD), BF16),
            vmem((4, 3, 2, BLOCK, THIRD), BF16),
            vmem((4, 3, SHARD_ROWS, LANES), BF16),
            vmem((4, 3, SHARD_ROWS, LANES), BF16),
            vmem((3, 384, THIRD), BF16),
            vmem((3, 384, THIRD), BF16),
            vmem((4, 2, BLOCK, THIRD), F32),
            vmem((3, 2, BLOCK, THIRD), F32),
            vmem((2, 2, SHARD_ROWS, LANES), F32),
            vmem((3, SHARD_ROWS, LANES), F32),
            vmem((4, 4, BLOCK, LANES), F32),
            vmem((3, 4, BLOCK, LANES), F32),
            vmem((2, 2, BLOCK, LANES), F32),
            vmem((3, BLOCK, LANES), F32),
            vmem((4, BLOCK, LANES), F32),
            vmem((3, BLOCK, LANES), F32),
            vmem((4, BLOCK, LANES), F32),
            vmem((3, BLOCK, LANES), F32),
            vmem((2, 4, 2, 3, BLOCK, LANES), BF16),
            vmem((TEACH, D), F32),
            pltpu.SemaphoreType.DMA((N_COPIES,)),
            pltpu.SemaphoreType.DMA((N_COPIES,)),
            pltpu.SemaphoreType.DMA((11,)),
        ],
        compiler_params=pltpu.CompilerParams(
            collective_id=0, has_side_effects=True, vmem_limit_bytes=50 * 2**20
        ),
        cost_estimate=pl.CostEstimate(
            flops=2 * D * D * (2 * TOKENS + TEACH), bytes_accessed=22 * 2**20, transcendentals=0
        ),
        name="exchange",
    )(*operands)


def finish_kernel(
    ctx_grad, teacher_out, gradient, weight, moment_one, moment_two, teacher_next,
    ctx_grad_o, weight_o, moment_one_o, moment_two_o, teacher_o, teacher_out_o,
    wo_v, oneo_v, twoo_v, out_sem,
):
    stores = []

    def store(src, dst):
        copy = pltpu.make_async_copy(src, dst, out_sem.at[len(stores)])
        copy.start()
        stores.append(copy)

    store(teacher_next, teacher_o)
    for r in range(4):
        rows = pl.ds(r * (TOKENS // 4), TOKENS // 4)
        store(ctx_grad.at[rows], ctx_grad_o.at[rows])
    for r in range(2):
        rows = pl.ds(r * (TEACH // 2), TEACH // 2)
        store(teacher_out.at[rows], teacher_out_o.at[rows])
    correct_one = 1.0 - beta_one**STEP
    correct_two = 1.0 - beta_two**STEP
    for r in range(4):
        rows = pl.ds(r * BLOCK, BLOCK)
        g, w = gradient[rows, :].astype(F32), weight[rows, :]
        one = beta_one * moment_one[rows, :] + (1.0 - beta_one) * g
        two = beta_two * moment_two[rows, :] + (1.0 - beta_two) * g * g
        update = one / correct_one / (jnp.sqrt(two / correct_two) + adam_eps) + decay_rate * w
        wo_v[rows, :] = w - learn_rate * update
        oneo_v[rows, :] = one
        twoo_v[rows, :] = two
        for src, dst in ((wo_v, weight_o), (oneo_v, moment_one_o), (twoo_v, moment_two_o)):
            store(src.at[rows], dst.at[rows])
    for copy in stores:
        copy.wait()


def finish(*operands):
    anywhere, near = pl.BlockSpec(memory_space=pl.ANY), pl.BlockSpec(memory_space=pltpu.VMEM)
    state = jax.ShapeDtypeStruct((SHARD_ROWS, D), F32)
    return pl.pallas_call(
        finish_kernel,
        out_shape=(
            jax.ShapeDtypeStruct((TOKENS, D), BF16), state, state, state, state,
            jax.ShapeDtypeStruct((TEACH, D), BF16),
        ),
        in_specs=[near] * 7,
        out_specs=(anywhere,) * 6,
        scratch_shapes=[pltpu.VMEM((SHARD_ROWS, D), F32)] * 3 + [pltpu.SemaphoreType.DMA((19,))],
        compiler_params=pltpu.CompilerParams(vmem_limit_bytes=24 * 2**20),
        cost_estimate=pl.CostEstimate(flops=10 * SHARD_ROWS * D, bytes_accessed=12 * 2**20, transcendentals=0),
        name="finish",
    )(*operands)


def body(student_ctx, out_grad, weight, moment_one, moment_two, teacher, teach_input, teach_ctx):
    results = communicate(
        student_ctx, out_grad, weight, moment_one, moment_two, teacher, teach_input, teach_ctx
    )
    return finish(*results)


def solution(mesh):
    return jax.shard_map(
        body,
        mesh=mesh,
        in_specs=(
            P(("replica", "shard"), None),
            P(("replica", "shard"), None),
            P("shard", None),
            P("shard", None),
            P("shard", None),
            P("shard", None),
            P(("replica", "shard"), None),
            P(("replica", "shard"), None),
        ),
        out_specs=(
            P(("replica", "shard"), None),
            P("shard", None),
            P("shard", None),
            P("shard", None),
            P("shard", None),
            P(("replica", "shard"), None),
        ),
        check_vma=False,
    )
```
